256 devices in a mesh: ctx: 64 (over z, x, core), head: 4 (over y).
Axes of the slice: x: 4, y: 4, z: 8, core: 2. Of those that a mesh axis runs over, the one named last changes fastest.
Arguments:
- queries: bfloat16 [65536, 4096], P('ctx', 'head'), may hold values from -6 to 6
- keys: bfloat16 [65536, 4096], P('ctx', 'head'), may hold values from -0.059814453 to 0.059814453
- values: bfloat16 [65536, 4096], P('ctx', 'head'), may hold values from -40 to 40
- log_decay: float32 [32, 65536], P('head', 'ctx'), may hold values from -1 to 0
- out_gain: float32 [4096], P('head'), may hold values from 0.1 to 1.9
- decode_map: int32 [256], P(('ctx', 'head')), may hold values from 0 to 255, each once
Outputs:
- out: bfloat16 [65536, 4096], P('ctx', 'head')
- decode_state: float32 [4096, 128], P(('ctx', 'head'))
The draws below stay inside these ranges and needn't reach their ends.
Inputs may be any that keep to these rules, and one draw needn't show every extreme that they name: `decode_map`: each slot names a different block.
All inputs are finite; a program needn't handle non-finite values.
Results may differ from the reference program's by a relative error of at most 0.0036.
Values sent between devices are 32-bit elements; how exact they have to be, the bound alone decides.
No kernel may reach another device: no remote copies, remote signals or barrier semaphores. Data moves between devices by JAX's collectives and lax.ppermute only.
A program may use at most 128 MiB of HBM per device.

```python
import math
import jax
import jax.numpy as jnp
from jax import lax

HEADS = 32
DK = 128
BLK = 256
TOKENS_PER_SHARD = 1024
TOKENS = 65536
SLOTS = 256
ROWBLK = 16


def draw_values(key, part):
    key = jax.random.fold_in(key, 7)
    first, second = jax.random.split(key, 2)
    columns = jnp.exp(jax.random.uniform(second, (HEADS * DK,), jnp.float32, 0.0, math.log(10.0)))
    base = jnp.clip(jax.random.normal(first, (TOKENS, HEADS * DK), jnp.float32), -4.0, 4.0)
    return jnp.clip(base * columns, -40.0, 40.0).astype(jnp.bfloat16)


def draw_log_decay(key, part):
    key = jax.random.fold_in(key, 13)
    parts = jax.random.split(key, 8)
    order = jax.random.permutation(parts[0], HEADS)
    fast_count = jax.random.randint(parts[1], (), HEADS // 4, HEADS // 2 + 1)
    fast = (order < fast_count)[:, None]
    quick = jnp.exp(jax.random.uniform(parts[2], (HEADS, 1), jnp.float32, math.log(1.0 / 50.0), math.log(1.0 / 30.0)))
    slow = jnp.exp(jax.random.uniform(parts[3], (HEADS, 1), jnp.float32, math.log(0.05), math.log(0.3))) / TOKENS
    base = jnp.where(fast, quick, slow)
    regions = jnp.exp(jax.random.uniform(parts[4], (HEADS, TOKENS // TOKENS_PER_SHARD, 1), jnp.float32, math.log(0.5), math.log(2.0)))
    regional = jnp.broadcast_to(regions, (HEADS, TOKENS // TOKENS_PER_SHARD, TOKENS_PER_SHARD)).reshape(HEADS, TOKENS)
    rough = jnp.exp(jax.random.uniform(parts[5], (HEADS, TOKENS), jnp.float32, math.log(0.5), math.log(2.0)))
    decay_speed = base * regional * rough
    spots = jax.random.randint(parts[6], (3, 1), 0, TOKENS)
    retained_decay = jax.random.uniform(parts[7], (3, HEADS), jnp.float32, 0.55, 0.8)
    matched_entries = (jnp.arange(TOKENS)[None, :] == spots).astype(jnp.float32)
    token_group_count = jnp.sum(matched_entries[:, None, :] * jnp.log(retained_decay)[:, :, None], axis=0)
    return -decay_speed + token_group_count


def levels(stream_key, extent, cuts, least, largest):
    def one(axis_at, shards_of):
        draws = jax.random.uniform(jax.random.fold_in(jax.random.fold_in(stream_key, 6), axis_at), (shards_of,), jnp.float32, least / len(cuts), largest / len(cuts))
        return jnp.repeat(jnp.exp(draws), extent[axis_at] // shards_of).reshape((-1,) + (1,) * (len(extent) - axis_at - 1))

    factor_of = one(*cuts[0])
    for cut in cuts[1:]:
        factor_of = factor_of * one(*cut)
    return factor_of


def noise(rng, dims, scale, reach, pieces=(), kind=jnp.bfloat16):
    gain = levels(rng, dims, pieces, -0.22, 0.18) if pieces else 1.0
    values = jax.random.normal(rng, dims, jnp.float32) * scale * gain
    return jnp.minimum(jnp.maximum(values, -reach), reach).astype(kind)


def setup_inputs(seed: int = 0) -> dict:
    key_list = jax.random.split(jax.random.key(seed), 7)
    queries = noise(key_list[0], (TOKENS, HEADS * DK), 1.0, 6.0, ((0, 64), (1, 4)))
    keys = noise(key_list[1], (TOKENS, HEADS * DK), 0.01, 0.059814453, ((0, 64), (1, 4)))
    values = draw_values(jax.random.fold_in(key_list[6], 71), 0)
    log_decay = draw_log_decay(jax.random.fold_in(key_list[6], 71), 0)
    out_gain = jnp.clip(1.0 + 0.18 * jax.random.normal(key_list[4], (HEADS * DK,), jnp.float32), 0.1, 1.9)
    decode_map = jax.random.permutation(key_list[5], SLOTS).astype(jnp.int32)
    return {"queries": queries, "keys": keys, "values": values, "log_decay": log_decay, "out_gain": out_gain, "decode_map": decode_map}


exact_mode = lax.Precision.HIGHEST

def reference(queries, keys, values, log_decay, out_gain, decode_map):
    blocks = TOKENS // BLK
    q_all = queries.reshape(blocks, BLK, HEADS, DK)
    k_all = keys.reshape(blocks, BLK, HEADS, DK)
    v_all = values.reshape(blocks, BLK, HEADS, DK)
    decay_all = log_decay.reshape(HEADS, blocks, BLK).transpose(1, 0, 2)
    positions = jnp.arange(BLK)
    causal = positions[:, None] >= positions[None, :]

    def step(state, inputs):
        q_block, k_block, v_block, decay_block = inputs
        cum = jnp.cumsum(decay_block, axis=1)
        total = cum[:, -1]
        q_float = q_block.astype(jnp.float32)
        k_float = k_block.astype(jnp.float32)
        v_float = v_block.astype(jnp.float32)
        scores = jnp.einsum('thd,shd->hts', q_float, k_float, precision=exact_mode)
        gap = cum[:, :, None] - cum[:, None, :]
        weights = jnp.where(causal[None], jnp.exp(jnp.where(causal[None], gap, 0.0)), 0.0)
        probs = lax.optimization_barrier((scores * weights).astype(jnp.bfloat16)).astype(jnp.float32)
        local = jnp.einsum('hts,shd->thd', probs, v_float, precision=exact_mode)
        carried = jnp.einsum('thd,hde->the', q_float, state, precision=exact_mode) * jnp.exp(cum).T[:, :, None]
        weighted = k_float * jnp.exp(total[:, None] - cum).T[:, :, None]
        gsum = jnp.einsum('shd,she->hde', weighted, v_float, precision=exact_mode)
        new_state = jnp.exp(total)[:, None, None] * state + gsum
        return (new_state, local + carried)
    start = jnp.zeros((HEADS, DK, DK), jnp.float32)
    final, attn = lax.scan(step, start, (q_all, k_all, v_all, decay_all))
    mean_sq = lax.optimization_barrier(jnp.mean(attn * attn, axis=-1, keepdims=True))
    normed = attn * lax.rsqrt(mean_sq + 1e-05) * out_gain.reshape(HEADS, DK)
    out = normed.reshape(TOKENS, HEADS * DK).astype(jnp.bfloat16)
    rows = final.reshape(SLOTS, ROWBLK, DK)
    decode_state = rows[decode_map].reshape(HEADS * DK, DK)
    return (out, decode_state)
```

```python
import functools

import jax
import jax.numpy as jnp
from jax import lax
from jax.experimental import pallas as pl
from jax.experimental.pallas import tpu as pltpu
from jax.sharding import PartitionSpec as P

BLK = 256
EXT = 8
f32 = jnp.float32
bf16 = jnp.bfloat16
SMEM = pl.BlockSpec(memory_space=pltpu.SMEM)
VMEM = pl.BlockSpec(memory_space=pltpu.VMEM)
PARAMS = pltpu.CompilerParams(vmem_limit_bytes=40 * 1024 * 1024)


def dot(a, b):
    return lax.dot_general(a, b, (((1,), (0,)), ((), ())), preferred_element_type=f32)


def split2(x):
    hi = x.astype(bf16)
    return hi, (x - hi.astype(f32)).astype(bf16)


def split3(x):
    hi = x.astype(bf16)
    rest = x - hi.astype(f32)
    mid = rest.astype(bf16)
    return hi, mid, (rest - mid.astype(f32)).astype(bf16)


def block_cums(ld):
    heads, tokens = ld.shape
    n = tokens // BLK
    row = lax.broadcasted_iota(jnp.int32, (BLK, BLK), 0)
    col = lax.broadcasted_iota(jnp.int32, (BLK, BLK), 1)
    tri = jnp.where(row <= col, 1.0, 0.0).astype(bf16)
    parts = []
    for j in range(n):
        parts += list(split3(ld[:, j * BLK : (j + 1) * BLK].astype(f32)))
    stacked = jnp.concatenate([p.astype(f32) for p in parts], axis=0).astype(bf16)
    sums = dot(stacked, tri)
    out = []
    for j in range(n):
        a = sums[(3 * j) * heads : (3 * j + 1) * heads]
        b = sums[(3 * j + 1) * heads : (3 * j + 2) * heads]
        c = sums[(3 * j + 2) * heads : (3 * j + 3) * heads]
        out.append(a + (b + c))
    return out


def summary_kernel(first, idx_ref, k_ref, v_ref, ld_ref, s_ref, w_ref, tot_ref):
    step = pl.program_id(0)
    heads, tokens = ld_ref.shape
    n = tokens // BLK
    half = heads // 2

    @pl.when(step == 0)
    def _():
        cums = block_cums(ld_ref[...])
        after = jnp.zeros((heads, 1), f32)
        for j in reversed(range(n)):
            total = cums[j][:, BLK - 1 : BLK]
            w_ref[:, j * BLK : (j + 1) * BLK] = jnp.exp(total - cums[j] + after)
            after = after + total
        tot_ref[...] = jnp.broadcast_to(after, tot_ref.shape)

    core = idx_ref[0]
    head = step + half * ((1 - core) if first else core)
    w = w_ref[pl.ds(head, 1), :]
    kt = k_ref[...].T.astype(f32) * w
    hi, lo = split2(kt)
    v = v_ref[...]
    s_ref[0, 0:128, :] = dot(hi, v) + dot(lo, v)
    s_ref[0, 128:136, :] = jnp.broadcast_to(tot_ref[pl.ds(head, 1), :], (EXT, 128))


def summary(first, idx, keys, values, ld):
    tokens, width = keys.shape
    heads = ld.shape[0]
    half = heads // 2

    def col(i, idx):
        return (0, i + half * ((1 - idx[0]) if first else idx[0]))

    return pl.pallas_call(
        functools.partial(summary_kernel, first),
        out_shape=jax.ShapeDtypeStruct((half, 128 + EXT, 128), f32),
        grid_spec=pltpu.PrefetchScalarGridSpec(
            num_scalar_prefetch=1,
            grid=(half,),
            in_specs=[
                pl.BlockSpec((tokens, 128), col),
                pl.BlockSpec((tokens, 128), col),
                pl.BlockSpec((heads, tokens), lambda i, idx: (0, 0)),
            ],
            out_specs=pl.BlockSpec((1, 128 + EXT, 128), lambda i, idx: (i, 0, 0)),
            scratch_shapes=[pltpu.VMEM((heads, tokens), f32), pltpu.VMEM((heads, 128), f32)],
        ),
        compiler_params=PARAMS,
        cost_estimate=pl.CostEstimate(flops=2 * 2 * half * tokens * 128 * 128, bytes_accessed=2 * tokens * width, transcendentals=0),
        name="summary_a" if first else "summary_b",
    )(idx, keys, values, ld)


def compose(early, late):
    scale = jnp.exp(late[1])
    return (scale[0:1] * early[0] + late[0], early[1] + late[1])


def parts(ref):
    return (ref[0:128, :], ref[128:136, :])


def pair_kernel(idx_ref, keep_ref, recv_ref, *outs):
    core, x = idx_ref[0], idx_ref[1]
    for d in range(4):
        j = x ^ d
        own = (keep_ref[j, 0:128, :], keep_ref[j, 128:136, :])
        got = (recv_ref[j, 0:128, :], recv_ref[j, 128:136, :])
        zero = core == 0
        early = tuple(jnp.where(zero, a, b) for a, b in zip(own, got))
        late = tuple(jnp.where(zero, b, a) for a, b in zip(own, got))
        state, decay = compose(early, late)
        outs[d][0:128, :] = state
        outs[d][128:136, :] = decay


def pick(x, j, refs):
    state, decay = parts(refs[0])
    for d in range(1, 4):
        here = (x ^ d) == j
        s, e = parts(refs[d])
        state, decay = jnp.where(here, s, state), jnp.where(here, e, decay)
    return state, decay


def slab_kernel(idx_ref, t0, t1, t2, t3, u_ref):
    x = idx_ref[1]
    refs = (t0, t1, t2, t3)
    total = pick(x, 0, refs)
    for j in range(1, 4):
        total = compose(total, pick(x, j, refs))
    u_ref[0:128, :] = total[0]
    u_ref[128:136, :] = total[1]


def round_kernel(bit, idx_ref, g_ref, r_ref, a_ref, g_out, a_out):
    late = idx_ref[bit] == 1
    g, r, a = parts(g_ref), parts(r_ref), parts(a_ref)
    early_part = tuple(jnp.where(late, p, q) for p, q in zip(r, g))
    late_part = tuple(jnp.where(late, p, q) for p, q in zip(g, r))
    state, decay = compose(early_part, late_part)
    g_out[0:128, :] = state
    g_out[128:136, :] = decay
    state, decay = compose(r, a)
    a_out[0:128, :] = jnp.where(late, state, a[0])
    a_out[128:136, :] = jnp.where(late, decay, a[1])


def back_kernel(idx_ref, g_ref, a_ref, t0, t1, t2, t3, *outs):
    x = idx_ref[1]
    refs = (t0, t1, t2, t3)
    before = [parts(a_ref)]
    for j in range(3):
        before.append(compose(before[-1], pick(x, j, refs)))
    for d in range(4):
        j = x ^ d
        state = before[0][0]
        for i in range(1, 4):
            state = jnp.where(j == i, before[i][0], state)
        outs[d][0:128, :] = state
        outs[d][128:256, :] = g_ref[0:128, :]


def spread_kernel(idx_ref, want_ref, m0, m1, m2, m3, keep_ref, recv_ref, own_ref, send_ref, slot_send, slot_keep):
    core, x, y = idx_ref[0], idx_ref[1], idx_ref[5]
    zero = core == 0
    refs = (m0, m1, m2, m3)
    for d in range(4):
        j = x ^ d
        chip = refs[d][0:128, :]
        s0 = jnp.where(zero, keep_ref[j, 0:128, :], recv_ref[j, 0:128, :])
        l0 = jnp.where(zero, keep_ref[j, 128:129, :], recv_ref[j, 128:129, :])
        second = jnp.exp(l0) * chip + s0
        own_ref[j] = jnp.where(zero, chip, second)
        send_ref[j] = jnp.where(zero, second, chip)
    for slot in range(8):
        want = want_ref[slot]
        mine = (want // 32) == (y * 2 + core)
        chip = ((want // 8) % 4) ^ x
        row = pl.multiple_of(128 + (want % 8) * 16, 16)
        rows = m0[pl.ds(row, 16), :]
        for d in range(1, 4):
            rows = jnp.where(chip == d, refs[d][pl.ds(row, 16), :], rows)
        rows = jnp.where(mine, rows, 0.0)
        if slot in (2, 3):
            slot_send[slot - 2] = rows
        elif slot in (6, 7):
            slot_send[slot - 4] = rows
        elif slot in (0, 1):
            slot_keep[slot] = rows
        else:
            slot_keep[slot - 2] = rows


def small(kernel, outs, name):
    def call(*args):
        n = args[0].size
        specs = [SMEM if a.dtype == jnp.int32 else VMEM for a in args]
        return pl.pallas_call(
            kernel,
            out_shape=[jax.ShapeDtypeStruct(s, f32) for s in outs],
            in_specs=specs,
            out_specs=[VMEM] * len(outs),
            compiler_params=PARAMS,
            name=name,
        )(*args)

    return call


def local_kernel(base, q_ref, k_ref, v_ref, ld_ref, attn_ref, e_ref, run_ref, off_ref):
    step = pl.program_id(0)
    count = q_ref.shape[1] // 128

    @pl.when(step == 0)
    def _():
        run_ref[...] = jnp.zeros_like(run_ref)
        off_ref[...] = jnp.zeros_like(off_ref)

    cum = block_cums(ld_ref[...])[0]
    total = cum[:, BLK - 1 : BLK]
    cum_t = cum.T
    e_in = jnp.exp(cum_t)
    off = off_ref[...]
    e_ref[...] = jnp.exp((cum + off[:, 0:1]).T)
    off_ref[...] = off + total
    tail = jnp.exp(total - cum)
    h2 = BLK // 2
    row = lax.broadcasted_iota(jnp.int32, (h2, h2), 0)
    col = lax.broadcasted_iota(jnp.int32, (h2, h2), 1)
    causal = row >= col
    for i in range(count):
        h = base + i
        cols = slice(i * 128, (i + 1) * 128)
        q, k, v = q_ref[:, cols], k_ref[:, cols], v_ref[:, cols]
        kt = k.T
        c_row = cum[h : h + 1, :]
        c_col = cum_t[:, h : h + 1]
        run = run_ref[i]
        hi, lo = split2(run)
        carried = dot(jnp.concatenate([q, q], axis=1), jnp.concatenate([hi, lo], axis=0))
        carried = carried * e_in[:, h : h + 1]
        for t in range(2):
            rows = slice(t * h2, (t + 1) * h2)
            scores = dot(q[rows], kt[:, : (t + 1) * h2])
            gap = c_col[rows] - c_row[:, rows]
            diag = jnp.where(causal, jnp.exp(jnp.where(causal, gap, 0.0)), 0.0) * scores[:, rows]
            if t == 0:
                probs = diag
            else:
                gap = c_col[rows] - c_row[:, :h2]
                probs = jnp.concatenate([jnp.exp(gap) * scores[:, :h2], diag], axis=1)
            attn_ref[rows, cols] = dot(probs.astype(bf16), v[: (t + 1) * h2]) + carried[rows]
        khi, klo = split2(kt.astype(f32) * tail[h : h + 1, :])
        run_ref[i] = run * jnp.exp(total[h : h + 1, :]) + (dot(khi, v) + dot(klo, v))


def local_part(part, count, queries, keys, values, ld):
    tokens, _ = keys.shape
    heads = ld.shape[0]
    tile = pl.BlockSpec((BLK, 128 * count), lambda j: (j, part))
    return pl.pallas_call(
        functools.partial(local_kernel, part * count),
        out_shape=[jax.ShapeDtypeStruct((tokens, 128 * count), f32), jax.ShapeDtypeStruct((tokens, heads), f32)],
        grid=(tokens // BLK,),
        in_specs=[tile, tile, tile, pl.BlockSpec((heads, BLK), lambda j: (0, j))],
        out_specs=[pl.BlockSpec((BLK, 128 * count), lambda j: (j, 0)), pl.BlockSpec((BLK, heads), lambda j: (j, 0))],
        scratch_shapes=[pltpu.VMEM((count, 128, 128), f32), pltpu.VMEM((heads, 128), f32)],
        compiler_params=PARAMS,
        cost_estimate=pl.CostEstimate(flops=count * tokens * 2 * 128 * (256 + 256 + 256), bytes_accessed=10 * tokens * 128 * count, transcendentals=count * tokens * 200),
        name="local_attn",
    )(queries, keys, values, ld)


def last_kernel(count, idx_ref, q_ref, e_ref, gain_ref, own_ref, recv_ref, *rest):
    attn_refs, out_ref, p_ref = rest[:-2], rest[-2], rest[-1]
    heads = p_ref.shape[0]
    half = heads // 2

    @pl.when(pl.program_id(0) == 0)
    def _():
        core = idx_ref[0]
        for h in range(heads):
            state = jnp.where(core == h // half, own_ref[h % half], recv_ref[h % half])
            hi, lo = split2(state)
            p_ref[h, 0:128, :] = hi
            p_ref[h, 128:256, :] = lo

    for h in range(heads):
        cols = slice(h * 128, (h + 1) * 128)
        q = q_ref[:, cols]
        sub = slice((h % count) * 128, (h % count + 1) * 128)
        carried = dot(jnp.concatenate([q, q], axis=1), p_ref[h])
        attn = attn_refs[h // count][:, sub] + carried * e_ref[:, h : h + 1]
        mean = jnp.mean(attn * attn, axis=1, keepdims=True)
        out_ref[:, cols] = (attn * lax.rsqrt(mean + 1e-5) * gain_ref[:, cols]).astype(bf16)


def last_part(count, idx, queries, e, gain, own, recv, attns):
    tokens, width = queries.shape
    heads = width // 128
    whole = pl.BlockSpec((heads // 2, 128, 128), lambda j: (0, 0, 0))
    return pl.pallas_call(
        functools.partial(last_kernel, count),
        out_shape=jax.ShapeDtypeStruct((tokens, width), bf16),
        grid=(tokens // BLK,),
        in_specs=[
            SMEM,
            pl.BlockSpec((BLK, width), lambda j: (j, 0)),
            pl.BlockSpec((BLK, heads), lambda j: (j, 0)),
            pl.BlockSpec((1, width), lambda j: (0, 0)),
            whole,
            whole,
        ]
        + [pl.BlockSpec((BLK, 128 * count), lambda j: (j, 0))] * len(attns),
        out_specs=pl.BlockSpec((BLK, width), lambda j: (j, 0)),
        scratch_shapes=[pltpu.VMEM((heads, 256, 128), bf16)],
        compiler_params=PARAMS,
        cost_estimate=pl.CostEstimate(flops=heads * tokens * 2 * 256 * 128, bytes_accessed=8 * tokens * width, transcendentals=tokens * heads),
        name="last",
    )(idx, queries, e, gain, own, recv, *attns)


def per_device(queries, keys, values, log_decay, out_gain, decode_map):
    ctx_size = lax.axis_size("ctx")
    head_size = lax.axis_size("head")

    def swap(a, mask):
        return lax.ppermute(a, "ctx", [(i, i ^ mask) for i in range(ctx_size)])

    def swap_y(a, mask):
        return lax.ppermute(a, "head", [(i, i ^ mask) for i in range(head_size)])

    at = lax.axis_index("ctx")
    y = lax.axis_index("head")
    core, x, z = at % 2, (at // 2) % 4, at // 8
    idx = jnp.stack([core, x, z & 1, (z >> 1) & 1, z >> 2, y]).astype(jnp.int32)

    ext = (128 + EXT, 128)
    send = summary(True, idx, keys, values, log_decay)
    recv = swap(send, 1)
    keep = summary(False, idx, keys, values, log_decay)

    w1 = jnp.concatenate([decode_map, swap(decode_map, 1)])
    w2 = jnp.concatenate([w1, swap_y(w1, 1)])
    want = jnp.concatenate([w2, swap_y(w2, 3)])

    t = small(pair_kernel, [ext] * 4, "pair")(idx, keep, recv)
    t = [t[0]] + [swap(t[d], 2 * d) for d in (1, 2, 3)]
    (g,) = small(slab_kernel, [ext], "slab")(idx, *t)
    a = jnp.zeros(ext, f32)
    for bit, mask in ((2, 8), (3, 16), (4, 48)):
        r = swap(g, mask)
        g, a = small(functools.partial(round_kernel, bit), [ext] * 2, "round")(idx, g, r, a)
    m = small(back_kernel, [(256, 128)] * 4, "back")(idx, g, a, *t)
    m = [m[0]] + [swap(m[d], 2 * d) for d in (1, 2, 3)]
    own, other, slot_send, slot_keep = small(
        spread_kernel, [(4, 128, 128)] * 2 + [(4, 16, 128)] * 2, "spread"
    )(idx, want, *m, keep, recv)
    other = swap(other, 1)

    slots = slot_keep + swap_y(slot_send, 1)
    slots = slots[0:2] + swap_y(slots[2:4], 3)
    decode_state = slots[0] + swap(slots[1], 1)

    count = 2
    locals_ = [local_part(i, count, queries, keys, values, log_decay) for i in range(8 // count)]
    out = last_part(
        count, idx, queries, locals_[0][1], out_gain.reshape(1, -1), own, other, [p[0] for p in locals_]
    )
    return (out, decode_state)


def solution(mesh):
    return jax.shard_map(
        per_device,
        mesh=mesh,
        in_specs=(
            P("ctx", "head"),
            P("ctx", "head"),
            P("ctx", "head"),
            P("head", "ctx"),
            P("head"),
            P(("ctx", "head")),
        ),
        out_specs=(P("ctx", "head"), P(("ctx", "head"), None)),
        check_vma=False,
    )
```

```python
import functools

import jax
import jax.numpy as jnp
from jax import lax
from jax.experimental import pallas as pl
from jax.experimental.pallas import tpu as pltpu
from jax.sharding import PartitionSpec as P

BLK = 256
EXT = 8
f32 = jnp.float32
bf16 = jnp.bfloat16
SMEM = pl.BlockSpec(memory_space=pltpu.SMEM)
VMEM = pl.BlockSpec(memory_space=pltpu.VMEM)
HBM = pl.BlockSpec(memory_space=pltpu.HBM)
ANY = pl.BlockSpec(memory_space=pl.ANY)
FAR_FIRST = (0, 2, 1, 3)
LOG2E = 1.4426950408889634
PARAMS = pltpu.CompilerParams(vmem_limit_bytes=40 * 1024 * 1024)


def dot(a, b):
    return lax.dot_general(a, b, (((1,), (0,)), ((), ())), preferred_element_type=f32)


def split2(x):
    hi = x.astype(bf16)
    return hi, (x - hi.astype(f32)).astype(bf16)


def split3(x):
    hi = x.astype(bf16)
    rest = x - hi.astype(f32)
    mid = rest.astype(bf16)
    return hi, mid, (rest - mid.astype(f32)).astype(bf16)


def block_cums(ld):
    heads, tokens = ld.shape
    n = tokens // BLK
    row = lax.broadcasted_iota(jnp.int32, (BLK, BLK), 0)
    col = lax.broadcasted_iota(jnp.int32, (BLK, BLK), 1)
    tri = jnp.where(row <= col, 1.0, 0.0).astype(bf16)
    parts = []
    for j in range(n):
        parts += list(split3(ld[:, j * BLK : (j + 1) * BLK].astype(f32)))
    stacked = jnp.concatenate([p.astype(f32) for p in parts], axis=0).astype(bf16)
    sums = dot(stacked, tri)
    out = []
    for j in range(n):
        a = sums[(3 * j) * heads : (3 * j + 1) * heads]
        b = sums[(3 * j + 1) * heads : (3 * j + 2) * heads]
        c = sums[(3 * j + 2) * heads : (3 * j + 3) * heads]
        out.append(a + (b + c))
    return out


def place():
    at = lax.axis_index("ctx")
    return at & 1, (at >> 1) & 3, at >> 3, lax.axis_index("head")


def kept_first(ld, core):
    half = ld.shape[0] // 2
    return jnp.where(core == 0, ld, jnp.concatenate([ld[half:], ld[:half]], axis=0))


def state_sum(k, v, w):
    kt = k.T.astype(f32) * w
    hi, lo = split2(kt)
    both = dot(jnp.concatenate([hi, lo], axis=0), v)
    return both[:128] + both[128:]


def write_sum(s_ref, i, state, tot_ref, h):
    s_ref[i, 0:128, :] = state
    heads = tot_ref.shape[0] - 8
    s_ref[i, 128:135, :] = jnp.broadcast_to(tot_ref[h : h + 1, :], (7, 128))
    s_ref[i, 135:136, :] = tot_ref[heads : heads + 1, :]


def send_kernel(k_hbm, v_hbm, ld_hbm, map_ref, s_ref, w_ref, tot_ref, k_ref, v_ref, ld_buf, sems, ld_sem):
    core = place()[0]
    heads, tokens = ld_buf.shape
    half = heads // 2
    ld_copy = pltpu.make_async_copy(ld_hbm, ld_buf, ld_sem)
    ld_copy.start()
    copies = {}

    def fetch(i):
        col = pl.multiple_of(((i + half * core) % heads) * 128, 128)
        copies[i] = [
            pltpu.make_async_copy(src.at[:, pl.ds(col, 128)], buf.at[i], sems.at[n, i])
            for n, (src, buf) in enumerate(((k_hbm, k_ref), (v_hbm, v_ref)))
        ]
        for copy in copies[i]:
            copy.start()

    for i in range(half, heads):
        fetch(i)
    ld_copy.wait()
    for i in range(half):
        fetch(i)
    ld = kept_first(ld_buf[...], core)
    n = tokens // BLK
    cums = block_cums(ld)
    after = jnp.zeros((heads, 1), f32)
    for j in reversed(range(n)):
        total = cums[j][:, BLK - 1 : BLK]
        w_ref[:, j * BLK : (j + 1) * BLK] = jnp.exp(total - cums[j] + after)
        after = after + total
    tot_ref[0:heads, :] = jnp.broadcast_to(after, (heads, 128))
    tot_ref[heads:, :] = jnp.full((8, 128), map_ref[0], jnp.int32).astype(f32)
    for i in range(half):
        h = i + half
        for copy in copies[h]:
            copy.wait()
        write_sum(s_ref, i, state_sum(k_ref[h], v_ref[h], w_ref[h : h + 1, :]), tot_ref, h)
    for i in range(half):
        for copy in copies[i]:
            copy.wait()


def keep_kernel(k_ref, v_ref, w_ref, tot_ref, s_ref):
    for i in range(s_ref.shape[0]):
        write_sum(s_ref, i, state_sum(k_ref[i], v_ref[i], w_ref[i : i + 1, :]), tot_ref, i)


def summaries(keys, values, ld, decode_map):
    tokens, _ = keys.shape
    heads = ld.shape[0]
    half = heads // 2
    out = jax.ShapeDtypeStruct((half, 128 + EXT, 128), f32)
    by_head = jax.ShapeDtypeStruct((heads, tokens, 128), bf16)
    cost = pl.CostEstimate(flops=2 * 2 * half * tokens * 128 * 128, bytes_accessed=2 * tokens * heads * 128, transcendentals=0)
    inputs = [pltpu.with_memory_space_constraint(a, pltpu.HBM) for a in (keys, values, ld)]
    send, w, tot, k_heads, v_heads = pl.pallas_call(
        send_kernel,
        out_shape=[
            out,
            jax.ShapeDtypeStruct((heads, tokens), f32),
            jax.ShapeDtypeStruct((heads + 8, 128), f32),
            by_head,
            by_head,
        ],
        in_specs=[HBM, HBM, HBM, SMEM],
        out_specs=[VMEM] * 5,
        scratch_shapes=[
            pltpu.VMEM((heads, tokens), f32),
            pltpu.SemaphoreType.DMA((2, heads)),
            pltpu.SemaphoreType.DMA(()),
        ],
        compiler_params=PARAMS,
        cost_estimate=cost,
        name="summary_send",
    )(*inputs, decode_map)
    keep = pl.pallas_call(
        keep_kernel,
        out_shape=out,
        in_specs=[VMEM] * 4,
        out_specs=VMEM,
        compiler_params=PARAMS,
        cost_estimate=cost,
        name="summary_keep",
    )(k_heads, v_heads, w, tot)
    return send, keep, k_heads, v_heads


def compose(early, late):
    scale = jnp.exp(late[1])
    return (scale[0:1] * early[0] + late[0], early[1] + late[1])


def parts(ref):
    return (ref[0:128, :], ref[128:136, :])


def pair_kernel(keep_ref, recv_ref, *outs):
    core, x, _, _ = place()
    zero = core == 0
    for n, d in enumerate(FAR_FIRST):
        j = x ^ d
        own = (keep_ref[j, 0:128, :], keep_ref[j, 128:136, :])
        got = (recv_ref[j, 0:128, :], recv_ref[j, 128:136, :])
        early = tuple(jnp.where(zero, a, b) for a, b in zip(own, got))
        late = tuple(jnp.where(zero, b, a) for a, b in zip(own, got))
        state, decay = compose(early, late)
        outs[n][0:128, :] = state
        outs[n][128:136, :] = decay
    outs[4][0:1, :] = keep_ref[0, 135:136, :]
    outs[4][1:2, :] = recv_ref[0, 135:136, :]
    outs[4][2:8, :] = jnp.zeros((6, 128), f32)


def pick(x, j, refs):
    state, decay = parts(refs[0])
    for n in range(1, 4):
        here = (x ^ FAR_FIRST[n]) == j
        s, e = parts(refs[n])
        state, decay = jnp.where(here, s, state), jnp.where(here, e, decay)
    return state, decay


def slab_kernel(t0, t1, t2, t3, u_ref):
    _, x, _, _ = place()
    refs = (t0, t1, t2, t3)
    total = pick(x, 0, refs)
    for j in range(1, 4):
        total = compose(total, pick(x, j, refs))
    u_ref[0:128, :] = total[0]
    u_ref[128:136, :] = total[1]


def want_kernel(want_ref, got_ref, w_ref):
    w_ref[0:2, :] = want_ref[0:2, :]
    w_ref[2:4, :] = got_ref[0:2, :]
    w_ref[4:8, :] = jnp.zeros((4, 128), f32)


def round_kernel(bit, g_ref, r_ref, *rest):
    a_ref = rest[0] if len(rest) == 3 else None
    g_out, a_out = rest[-2:]
    late = ((place()[2] >> bit) & 1) == 1
    g, r = parts(g_ref), parts(r_ref)
    early_part = tuple(jnp.where(late, p, q) for p, q in zip(r, g))
    late_part = tuple(jnp.where(late, p, q) for p, q in zip(g, r))
    state, decay = compose(early_part, late_part)
    g_out[0:128, :] = state
    g_out[128:136, :] = decay
    a = parts(a_ref) if a_ref is not None else tuple(jnp.zeros_like(p) for p in r)
    state, decay = compose(r, a)
    a_out[0:128, :] = jnp.where(late, state, a[0])
    a_out[128:136, :] = jnp.where(late, decay, a[1])


def back_kernel(g_ref, a_ref, t0, t1, t2, t3, *outs):
    _, x, _, _ = place()
    refs = (t0, t1, t2, t3)
    before = [parts(a_ref)]
    for j in range(3):
        before.append(compose(before[-1], pick(x, j, refs)))
    for n, d in enumerate(FAR_FIRST):
        j = x ^ d
        state = before[0][0]
        for i in range(1, 4):
            state = jnp.where(j == i, before[i][0], state)
        outs[n][0:128, :] = state
        outs[n][128:256, :] = g_ref[0:128, :]


def spread_kernel(want_a, want_b, m0, m1, m2, m3, keep_ref, recv_ref, own_ref, send_ref, slot_ref):
    core, x, _, y = place()
    zero = core == 0
    refs = (m0, m1, m2, m3)
    for n, d in enumerate(FAR_FIRST):
        j = x ^ d
        chip = refs[n][0:128, :]
        s0 = jnp.where(zero, keep_ref[j, 0:128, :], recv_ref[j, 0:128, :])
        l0 = jnp.where(zero, keep_ref[j, 128:129, :], recv_ref[j, 128:129, :])
        second = jnp.exp(l0) * chip + s0
        own_ref[j] = jnp.where(zero, chip, second)
        send_ref[j, 0:128, :] = jnp.where(zero, second, chip)
    base = (y * 2 + core) * 32
    for slot in range(8):
        away = (0, 1, 3, 2)[slot // 2]
        want = (want_a if slot < 4 else want_b)[slot % 4 : slot % 4 + 1, :]
        rows = jnp.zeros((16, 128), f32)
        for n, d in enumerate(FAR_FIRST):
            for r in range(8):
                number = (base + (x ^ d) * 8 + r).astype(f32)
                rows = jnp.where(want == number, refs[n][128 + r * 16 : 144 + r * 16, :], rows)
        if slot % 2:
            send_ref[away, 128:144, :] = rows
        else:
            slot_ref[away] = rows


def merge_kernel(slot_ref, got_ref, send_ref, near_ref, far_ref):
    both = [slot_ref[d] + got_ref[d, 128:144, :] for d in range(4)]
    near_ref[...], far_ref[...] = both[0], both[3]
    send_ref[0], send_ref[1] = both[1], both[2]


def slots_kernel(got_ref, a_ref, b_ref, near_ref, far_ref):
    near_ref[...] = a_ref[...] + got_ref[0]
    far_ref[...] = b_ref[...] + got_ref[1]


def add_kernel(a_ref, b_ref, out_ref):
    out_ref[...] = a_ref[...] + b_ref[...]


def small(kernel, outs, name, after=()):
    def call(*args):
        def body(*refs):
            kernel(*refs[: len(args)], *refs[len(args) + len(after) :])

        return pl.pallas_call(
            body,
            out_shape=[jax.ShapeDtypeStruct(s, f32) for s in outs],
            in_specs=[VMEM] * len(args) + [ANY] * len(after),
            out_specs=[VMEM] * len(outs),
            compiler_params=PARAMS,
            name=name,
        )(*args, *after)

    return call


def prep_kernel(ld_ref, cr_ref, ct_ref):
    core = place()[0]
    ld = kept_first(ld_ref[...], core)
    for j, cum in enumerate(block_cums(ld)):
        rows = slice(j * BLK, (j + 1) * BLK)
        cum = cum * LOG2E
        cr_ref[:, rows] = cum
        ct_ref[rows, :] = cum.T


def local_kernel(heads, q_ref, k_ref, v_ref, cr_ref, ct_ref, *rest):
    core = place()[0]
    total_heads, tokens = cr_ref.shape
    outs, scaled = rest[: len(heads)], rest[len(heads) :]
    h2 = BLK // 2
    row = lax.broadcasted_iota(jnp.int32, (h2, h2), 0)
    col = lax.broadcasted_iota(jnp.int32, (h2, h2), 1)
    causal = row >= col
    for i, out, qs in zip(heads, outs, scaled):
        at = pl.multiple_of(((i + total_heads // 2 * core) % total_heads) * 128, 128)
        run = None
        off = jnp.zeros((1, 1), f32)
        for j in range(tokens // BLK):
            rows = slice(j * BLK, (j + 1) * BLK)
            q, k, v = q_ref[rows, pl.ds(at, 128)], k_ref[i, rows, :], v_ref[i, rows, :]
            c_row = cr_ref[i : i + 1, rows]
            c_col = ct_ref[rows, i : i + 1]
            total = c_row[:, BLK - 1 : BLK]
            decay = jnp.broadcast_to(jnp.exp2(c_col), (BLK, 128))
            hi, lo = split2(q.astype(f32) * (decay * jnp.exp2(off)))
            qs[rows, 0:128] = hi
            qs[rows, 128:256] = lo
            off = off + total
            for t in range(2):
                part = slice(t * h2, (t + 1) * h2)
                seen = (t + 1) * h2
                scores = lax.dot_general(q[part], k[:seen], (((1,), (1,)), ((), ())), preferred_element_type=f32)
                gap = c_col[part] - c_row[:, :seen]
                inner = jnp.where(causal, jnp.exp2(jnp.where(causal, gap[:, t * h2 :], 0.0)), 0.0)
                weights = inner if t == 0 else jnp.concatenate([jnp.exp2(gap[:, :h2]), inner], axis=1)
                attn = dot((scores * weights).astype(bf16), v[:seen])
                if run is not None:
                    twice = jnp.concatenate([q[part], q[part]], axis=1)
                    attn = attn + dot(twice, halves) * decay[part]
                out[j * BLK + t * h2 : j * BLK + seen, :] = attn
            if j + 1 < tokens // BLK:
                new = state_sum(k, v, jnp.exp2(total - c_row))
                run = new if run is None else run * jnp.exp2(total) + new
                halves = jnp.concatenate(split2(run), axis=0)


def local_part(heads, queries, keys, values, cr, ct, after):
    tokens = queries.shape[0]
    n = len(heads)

    def body(*refs):
        local_kernel(heads, *refs[:5], *refs[5 + len(after) :])

    return pl.pallas_call(
        body,
        out_shape=[jax.ShapeDtypeStruct((tokens, 128), f32)] * n + [jax.ShapeDtypeStruct((tokens, 256), bf16)] * n,
        in_specs=[VMEM] * 5 + [ANY] * len(after),
        out_specs=[VMEM] * 2 * n,
        compiler_params=PARAMS,
        cost_estimate=pl.CostEstimate(flops=n * tokens * 2 * 128 * (256 + 256 + 256), bytes_accessed=10 * tokens * 128 * n, transcendentals=n * tokens * 200),
        name="local_attn",
    )(queries, keys, values, cr, ct, *after)


def last_kernel(heads, gain_ref, p_ref, *rest):
    half, n = p_ref.shape[0], len(heads)
    attn_refs, q_refs = rest[:n], rest[n : 2 * n]
    out_ref, mark_ref, buf, sems = rest[-4:]
    mark_ref[...] = jnp.zeros(mark_ref.shape, f32)
    first = pl.multiple_of(((heads[0] + half * place()[0]) % (2 * half)) * 128, 128 * n)
    tokens = buf.shape[0]
    state = []
    for i in heads:
        hi, lo = split2(p_ref[i % half, 0:128, :])
        state.append((jnp.concatenate([hi, hi], axis=0), lo))
    copies = []
    for j in range(tokens // BLK):
        rows = slice(j * BLK, (j + 1) * BLK)
        for i in range(n):
            at = pl.multiple_of(first + i * 128, 128)
            both = q_refs[i][rows, :]
            carried = dot(both, state[i][0]) + dot(both[:, :128], state[i][1])
            attn = attn_refs[i][rows, :] + carried
            mean = jnp.mean(attn * attn, axis=1, keepdims=True)
            normed = attn * lax.rsqrt(mean + 1e-5) * gain_ref[:, pl.ds(at, 128)]
            buf[rows, i * 128 : (i + 1) * 128] = normed.astype(bf16)
        copy = pltpu.make_async_copy(buf.at[rows, :], out_ref.at[rows, pl.ds(first, n * 128)], sems.at[j])
        copy.start()
        copies.append(copy)
    for copy in copies:
        copy.wait()


def last_part(heads, gain, state, attn, scaled, out=None, after=()):
    n = len(heads)
    tokens, width = attn[0].shape[0], gain.shape[1]
    given = ([] if out is None else [out]) + list(after)
    return pl.pallas_call(
        functools.partial(last_kernel, heads),
        out_shape=[jax.ShapeDtypeStruct((tokens, width), bf16), jax.ShapeDtypeStruct((8, 128), f32)],
        in_specs=[VMEM] * (2 + 2 * n) + [ANY] * len(given),
        out_specs=[HBM, VMEM],
        scratch_shapes=[pltpu.VMEM((tokens, n * 128), bf16), pltpu.SemaphoreType.DMA((tokens // BLK,))],
        input_output_aliases={} if out is None else {2 + 2 * n: 0},
        compiler_params=PARAMS,
        cost_estimate=pl.CostEstimate(flops=n * tokens * 2 * 384 * 128, bytes_accessed=10 * tokens * 128 * n, transcendentals=tokens * n),
        name="last",
    )(gain, state, *[attn[i] for i in heads], *[scaled[i] for i in heads], *given)


def per_device(queries, keys, values, log_decay, out_gain, decode_map):
    ctx_size = lax.axis_size("ctx")
    head_size = lax.axis_size("head")

    def swap(a, mask):
        return lax.ppermute(a, "ctx", [(i, i ^ mask) for i in range(ctx_size)])

    def swap_y(a, mask):
        return lax.ppermute(a, "head", [(i, i ^ mask) for i in range(head_size)])

    tokens = queries.shape[0]
    heads = log_decay.shape[0]
    half = heads // 2
    ext = (128 + EXT, 128)
    send, keep, k_heads, v_heads = summaries(keys, values, log_decay, decode_map)
    recv = swap(send, 1)

    *t, want = small(pair_kernel, [ext] * 4 + [(8, 128)], "pair")(keep, recv)
    cr, ct = small(prep_kernel, [(heads, tokens), (tokens, heads)], "prep", (t[0],))(log_decay)
    attn, scaled = [None] * heads, [None] * heads

    def local(which, *after):
        got = local_part(which, queries, k_heads, v_heads, cr, ct, after)
        for n, i in enumerate(which):
            attn[i], scaled[i] = got[n], got[n + len(which)]
        return tuple(got[: len(which)])

    t = [t[0]] + [swap(a, 2 * d) for a, d in zip(t[1:], FAR_FIRST[1:])]
    done = local((0,), t[0])
    (g,) = small(slab_kernel, [ext], "slab", done)(*t)
    a = []
    plan = ((0, 8, (1, 2)), (1, 16, (3, 4)), (2, 48, (5, 6)))
    for bit, mask, which in plan:
        r = swap(g, mask)
        done = local(which, g)
        if bit == 0:
            want_y = swap_y(want, 1)
        if bit == 1:
            done = done + (want_y,)
        g, *a = small(functools.partial(round_kernel, bit), [ext] * 2, "round", done)(g, r, *a)
    m = small(back_kernel, [(256, 128)] * 4, "back")(g, *a, *t)
    (want_a,) = small(want_kernel, [(8, 128)], "want", (m[0],))(want, want_y)
    want_b = swap_y(want_a, 3)
    done = local((7,), m[0])
    m = [m[0]] + [swap(a, 2 * d) for a, d in zip(m[1:], FAR_FIRST[1:])]
    own, other, slots = small(
        spread_kernel, [(half, 128, 128), (half, 144, 128), (4, 16, 128)], "spread", done
    )(want_a, want_b, *m, keep, recv)
    other = swap(other, 1)

    gain = out_gain.reshape(1, -1)
    out, mark = last_part((0, 1), gain, own, attn, scaled)
    slot_send, near, far = small(merge_kernel, [(2, 16, 128), (16, 128), (16, 128)], "merge", (mark,))(slots, other)
    got = swap_y(slot_send, 1)
    out, mark = last_part((2, 3), gain, own, attn, scaled, out, (near,))
    near, far = small(slots_kernel, [(16, 128)] * 2, "slots", (mark,))(got, near, far)
    got = swap_y(far, 3)
    out, mark = last_part((4, 5, 6, 7), gain, other, attn, scaled, out, (near,))
    (decode_state,) = small(add_kernel, [(16, 128)], "sum", (mark,))(near, got)
    return (out, decode_state)


def solution(mesh):
    return jax.shard_map(
        per_device,
        mesh=mesh,
        in_specs=(
            P("ctx", "head"),
            P("ctx", "head"),
            P("ctx", "head"),
            P("head", "ctx"),
            P("head"),
            P(("ctx", "head")),
        ),
        out_specs=(P("ctx", "head"), P(("ctx", "head"), None)),
        check_vma=False,
    )
```

```python
import functools

import jax
import jax.numpy as jnp
from jax import lax
from jax.experimental import pallas as pl
from jax.experimental.pallas import tpu as pltpu
from jax.sharding import PartitionSpec as P

BLK = 256
EXT = 8
f32 = jnp.float32
bf16 = jnp.bfloat16
SMEM = pl.BlockSpec(memory_space=pltpu.SMEM)
VMEM = pl.BlockSpec(memory_space=pltpu.VMEM)
HBM = pl.BlockSpec(memory_space=pltpu.HBM)
ANY = pl.BlockSpec(memory_space=pl.ANY)
FAR_FIRST = (0, 2, 1, 3)
LOG2E = 1.4426950408889634
PARAMS = pltpu.CompilerParams(vmem_limit_bytes=40 * 1024 * 1024)


def dot(a, b):
    return lax.dot_general(a, b, (((1,), (0,)), ((), ())), preferred_element_type=f32)


def split2(x):
    hi = x.astype(bf16)
    return hi, (x - hi.astype(f32)).astype(bf16)


def split3(x):
    hi = x.astype(bf16)
    rest = x - hi.astype(f32)
    mid = rest.astype(bf16)
    return hi, mid, (rest - mid.astype(f32)).astype(bf16)


def block_cums(ld):
    heads, tokens = ld.shape
    n = tokens // BLK
    row = lax.broadcasted_iota(jnp.int32, (BLK, BLK), 0)
    col = lax.broadcasted_iota(jnp.int32, (BLK, BLK), 1)
    tri = jnp.where(row <= col, 1.0, 0.0).astype(bf16)
    parts = []
    for j in range(n):
        parts += list(split3(ld[:, j * BLK : (j + 1) * BLK].astype(f32)))
    stacked = jnp.concatenate([p.astype(f32) for p in parts], axis=0).astype(bf16)
    sums = dot(stacked, tri)
    out = []
    for j in range(n):
        a = sums[(3 * j) * heads : (3 * j + 1) * heads]
        b = sums[(3 * j + 1) * heads : (3 * j + 2) * heads]
        c = sums[(3 * j + 2) * heads : (3 * j + 3) * heads]
        out.append(a + (b + c))
    return out


def place():
    at = lax.axis_index("ctx")
    return at & 1, (at >> 1) & 3, at >> 3, lax.axis_index("head")


def kept_first(ld, core):
    half = ld.shape[0] // 2
    return jnp.where(core == 0, ld, jnp.concatenate([ld[half:], ld[:half]], axis=0))


def head_column(i, heads):
    return pl.multiple_of(((i + heads // 2 * place()[0]) % heads) * 128, 128)


def state_sum(k, v, w):
    kt = k.T.astype(f32) * w
    hi, lo = split2(kt)
    both = dot(jnp.concatenate([hi, lo], axis=0), v)
    return both[:128] + both[128:]


def write_sum(s_ref, i, state, tot_ref, h):
    s_ref[i, 0:128, :] = state
    heads = tot_ref.shape[0] - 8
    s_ref[i, 128:135, :] = jnp.broadcast_to(tot_ref[h : h + 1, :], (7, 128))
    s_ref[i, 135:136, :] = tot_ref[heads : heads + 1, :]


def send_kernel(k_hbm, v_hbm, ld_hbm, map_ref, s_ref, w_ref, tot_ref, k_ref, v_ref, ld_buf, sems, ld_sem):
    core = place()[0]
    heads, tokens = ld_buf.shape
    half = heads // 2
    ld_copy = pltpu.make_async_copy(ld_hbm, ld_buf, ld_sem)
    ld_copy.start()
    def fetch(side):
        cols = pl.ds(pl.multiple_of(((side + core) % 2) * half * 128, half * 128), half * 128)
        copies = []
        for r in range(sems.shape[2]):
            rows = pl.ds(r * (tokens // sems.shape[2]), tokens // sems.shape[2])
            for n, (src, buf) in enumerate(((k_hbm, k_ref), (v_hbm, v_ref))):
                copies.append(pltpu.make_async_copy(src.at[rows, cols], buf.at[rows, cols], sems.at[n, side, r]))
        for copy in copies:
            copy.start()
        return copies

    sent = fetch(1)
    ld_copy.wait()
    kept = fetch(0)
    ld = kept_first(ld_buf[...], core)
    n = tokens // BLK
    cums = block_cums(ld)
    after = jnp.zeros((heads, 1), f32)
    for j in reversed(range(n)):
        total = cums[j][:, BLK - 1 : BLK]
        w_ref[:, j * BLK : (j + 1) * BLK] = jnp.exp(total - cums[j] + after)
        after = after + total
    tot_ref[0:heads, :] = jnp.broadcast_to(after, (heads, 128))
    tot_ref[heads:, :] = jnp.full((8, 128), map_ref[0], jnp.int32).astype(f32)
    for copy in sent:
        copy.wait()
    for i in range(half):
        h = i + half
        cols = pl.ds(head_column(h, heads), 128)
        write_sum(s_ref, i, state_sum(k_ref[:, cols], v_ref[:, cols], w_ref[h : h + 1, :]), tot_ref, h)
    for copy in kept:
        copy.wait()


def keep_kernel(k_ref, v_ref, w_ref, tot_ref, s_ref):
    for i in range(s_ref.shape[0]):
        cols = pl.ds(head_column(i, 2 * s_ref.shape[0]), 128)
        write_sum(s_ref, i, state_sum(k_ref[:, cols], v_ref[:, cols], w_ref[i : i + 1, :]), tot_ref, i)


def summaries(keys, values, ld, decode_map):
    tokens, _ = keys.shape
    heads = ld.shape[0]
    half = heads // 2
    out = jax.ShapeDtypeStruct((half, 128 + EXT, 128), f32)
    cost = pl.CostEstimate(flops=2 * 2 * half * tokens * 128 * 128, bytes_accessed=2 * tokens * heads * 128, transcendentals=0)
    inputs = [pltpu.with_memory_space_constraint(a, pltpu.HBM) for a in (keys, values, ld)]
    send, w, tot, k_heads, v_heads = pl.pallas_call(
        send_kernel,
        out_shape=[
            out,
            jax.ShapeDtypeStruct((heads, tokens), f32),
            jax.ShapeDtypeStruct((heads + 8, 128), f32),
            jax.ShapeDtypeStruct(keys.shape, bf16),
            jax.ShapeDtypeStruct(keys.shape, bf16),
        ],
        in_specs=[HBM, HBM, HBM, SMEM],
        out_specs=[VMEM] * 5,
        scratch_shapes=[
            pltpu.VMEM((heads, tokens), f32),
            pltpu.SemaphoreType.DMA((2, 2, 1)),
            pltpu.SemaphoreType.DMA(()),
        ],
        compiler_params=PARAMS,
        cost_estimate=cost,
        name="summary_send",
    )(*inputs, decode_map)
    keep = pl.pallas_call(
        keep_kernel,
        out_shape=out,
        in_specs=[VMEM] * 4,
        out_specs=VMEM,
        compiler_params=PARAMS,
        cost_estimate=cost,
        name="summary_keep",
    )(k_heads, v_heads, w, tot)
    return send, keep, k_heads, v_heads


def compose(early, late):
    scale = jnp.exp(late[1])
    return (scale[0:1] * early[0] + late[0], early[1] + late[1])


def parts(ref):
    return (ref[0:128, :], ref[128:136, :])


def pair_kernel(keep_ref, recv_ref, *outs):
    core, x, _, _ = place()
    zero = core == 0
    for n, d in enumerate(FAR_FIRST):
        j = x ^ d
        own = (keep_ref[j, 0:128, :], keep_ref[j, 128:136, :])
        got = (recv_ref[j, 0:128, :], recv_ref[j, 128:136, :])
        early = tuple(jnp.where(zero, a, b) for a, b in zip(own, got))
        late = tuple(jnp.where(zero, b, a) for a, b in zip(own, got))
        state, decay = compose(early, late)
        outs[n][0:128, :] = state
        outs[n][128:136, :] = decay
    outs[4][0:1, :] = keep_ref[0, 135:136, :]
    outs[4][1:2, :] = recv_ref[0, 135:136, :]
    outs[4][2:8, :] = jnp.zeros((6, 128), f32)


def pick(x, j, refs):
    state, decay = parts(refs[0])
    for n in range(1, 4):
        here = (x ^ FAR_FIRST[n]) == j
        s, e = parts(refs[n])
        state, decay = jnp.where(here, s, state), jnp.where(here, e, decay)
    return state, decay


def slab_kernel(t0, t1, t2, t3, u_ref):
    _, x, _, _ = place()
    refs = (t0, t1, t2, t3)
    total = pick(x, 0, refs)
    for j in range(1, 4):
        total = compose(total, pick(x, j, refs))
    u_ref[0:128, :] = total[0]
    u_ref[128:136, :] = total[1]


def want_kernel(want_ref, got_ref, w_ref):
    w_ref[0:2, :] = want_ref[0:2, :]
    w_ref[2:4, :] = got_ref[0:2, :]
    w_ref[4:8, :] = jnp.zeros((4, 128), f32)


def round_kernel(bit, g_ref, r_ref, *rest):
    a_ref = rest[0] if len(rest) == 3 else None
    g_out, a_out = rest[-2:]
    late = ((place()[2] >> bit) & 1) == 1
    g, r = parts(g_ref), parts(r_ref)
    early_part = tuple(jnp.where(late, p, q) for p, q in zip(r, g))
    late_part = tuple(jnp.where(late, p, q) for p, q in zip(g, r))
    state, decay = compose(early_part, late_part)
    g_out[0:128, :] = state
    g_out[128:136, :] = decay
    a = parts(a_ref) if a_ref is not None else tuple(jnp.zeros_like(p) for p in r)
    state, decay = compose(r, a)
    a_out[0:128, :] = jnp.where(late, state, a[0])
    a_out[128:136, :] = jnp.where(late, decay, a[1])


def back_kernel(g_ref, a_ref, t0, t1, t2, t3, *outs):
    _, x, _, _ = place()
    refs = (t0, t1, t2, t3)
    before = [parts(a_ref)]
    for j in range(3):
        before.append(compose(before[-1], pick(x, j, refs)))
    for n, d in enumerate(FAR_FIRST):
        j = x ^ d
        state = before[0][0]
        for i in range(1, 4):
            state = jnp.where(j == i, before[i][0], state)
        outs[n][0:128, :] = state
        outs[n][128:256, :] = g_ref[0:128, :]


def spread_kernel(want_a, want_b, m0, m1, m2, m3, keep_ref, recv_ref, own_ref, send_ref, slot_ref):
    core, x, _, y = place()
    zero = core == 0
    refs = (m0, m1, m2, m3)
    for n, d in enumerate(FAR_FIRST):
        j = x ^ d
        chip = refs[n][0:128, :]
        s0 = jnp.where(zero, keep_ref[j, 0:128, :], recv_ref[j, 0:128, :])
        l0 = jnp.where(zero, keep_ref[j, 128:129, :], recv_ref[j, 128:129, :])
        second = jnp.exp(l0) * chip + s0
        own_ref[j] = jnp.where(zero, chip, second)
        send_ref[j, 0:128, :] = jnp.where(zero, second, chip)
    base = (y * 2 + core) * 32
    for slot in range(8):
        away = (0, 1, 3, 2)[slot // 2]
        want = (want_a if slot < 4 else want_b)[slot % 4 : slot % 4 + 1, :]
        rows = jnp.zeros((16, 128), f32)
        for n, d in enumerate(FAR_FIRST):
            for r in range(8):
                number = (base + (x ^ d) * 8 + r).astype(f32)
                rows = jnp.where(want == number, refs[n][128 + r * 16 : 144 + r * 16, :], rows)
        if slot % 2:
            send_ref[away, 128:144, :] = rows
        else:
            slot_ref[away] = rows


def merge_kernel(slot_ref, got_ref, send_ref, near_ref, far_ref):
    both = [slot_ref[d] + got_ref[d, 128:144, :] for d in range(4)]
    near_ref[...], far_ref[...] = both[0], both[3]
    send_ref[0], send_ref[1] = both[1], both[2]


def slots_kernel(got_ref, a_ref, b_ref, near_ref, far_ref):
    near_ref[...] = a_ref[...] + got_ref[0]
    far_ref[...] = b_ref[...] + got_ref[1]


def add_kernel(a_ref, b_ref, out_ref):
    out_ref[...] = a_ref[...] + b_ref[...]


def small(kernel, outs, name, after=()):
    def call(*args):
        def body(*refs):
            kernel(*refs[: len(args)], *refs[len(args) + len(after) :])

        return pl.pallas_call(
            body,
            out_shape=[jax.ShapeDtypeStruct(s, f32) for s in outs],
            in_specs=[VMEM] * len(args) + [ANY] * len(after),
            out_specs=[VMEM] * len(outs),
            compiler_params=PARAMS,
            name=name,
        )(*args, *after)

    return call


def prep_kernel(ld_ref, cr_ref, ct_ref):
    core = place()[0]
    ld = kept_first(ld_ref[...], core)
    for j, cum in enumerate(block_cums(ld)):
        rows = slice(j * BLK, (j + 1) * BLK)
        cum = cum * LOG2E
        cr_ref[:, rows] = cum
        ct_ref[rows, :] = cum.T


def local_kernel(heads, q_ref, k_ref, v_ref, cr_ref, ct_ref, *rest):
    total_heads, tokens = cr_ref.shape
    outs, scaled = rest[: len(heads)], rest[len(heads) :]
    h2 = BLK // 2
    row = lax.broadcasted_iota(jnp.int32, (h2, h2), 0)
    col = lax.broadcasted_iota(jnp.int32, (h2, h2), 1)
    causal = row >= col
    for i, out, qs in zip(heads, outs, scaled):
        at = head_column(i, total_heads)
        run = None
        off = jnp.zeros((1, 1), f32)
        for j in range(tokens // BLK):
            rows = slice(j * BLK, (j + 1) * BLK)
            q, k, v = q_ref[rows, pl.ds(at, 128)], k_ref[rows, pl.ds(at, 128)], v_ref[rows, pl.ds(at, 128)]
            c_row = cr_ref[i : i + 1, rows]
            c_col = ct_ref[rows, i : i + 1]
            total = c_row[:, BLK - 1 : BLK]
            decay = jnp.broadcast_to(jnp.exp2(c_col), (BLK, 128))
            hi, lo = split2(q.astype(f32) * (decay * jnp.exp2(off)))
            qs[rows, 0:128] = hi
            qs[rows, 128:256] = lo
            off = off + total
            scores = lax.dot_general(q, k, (((1,), (1,)), ((), ())), preferred_element_type=f32)
            gap = c_col - c_row
            top = jnp.where(causal, jnp.exp2(gap[:h2, :h2]) * scores[:h2, :h2], 0.0)
            low = jnp.exp2(gap[h2:, :h2]) * scores[h2:, :h2]
            end = jnp.where(causal, jnp.exp2(gap[h2:, h2:]) * scores[h2:, h2:], 0.0)
            left = jnp.concatenate([top.astype(bf16), low.astype(bf16)], axis=0)
            right = jnp.concatenate([jnp.zeros((h2, h2), bf16), end.astype(bf16)], axis=0)
            mixed = [jnp.concatenate([left, right], axis=1)]
            more = j + 1 < tokens // BLK
            if more:
                mixed += split2(k.T.astype(f32) * jnp.exp2(total - c_row))
            mixed = dot(jnp.concatenate(mixed, axis=0), v)
            attn = mixed[:BLK]
            if run is not None:
                attn = attn + dot(jnp.concatenate([q, q], axis=1), halves) * decay
            out[rows, :] = attn
            if more:
                new = mixed[BLK : BLK + 128] + mixed[BLK + 128 :]
                run = new if run is None else run * jnp.exp2(total) + new
                halves = jnp.concatenate(split2(run), axis=0)


def local_part(heads, queries, keys, values, cr, ct, after):
    tokens = queries.shape[0]
    n = len(heads)

    def body(*refs):
        local_kernel(heads, *refs[:5], *refs[5 + len(after) :])

    return pl.pallas_call(
        body,
        out_shape=[jax.ShapeDtypeStruct((tokens, 128), f32)] * n + [jax.ShapeDtypeStruct((tokens, 256), bf16)] * n,
        in_specs=[VMEM] * 5 + [ANY] * len(after),
        out_specs=[VMEM] * 2 * n,
        compiler_params=PARAMS,
        cost_estimate=pl.CostEstimate(flops=n * tokens * 2 * 128 * (256 + 256 + 256), bytes_accessed=10 * tokens * 128 * n, transcendentals=n * tokens * 200),
        name="local_attn",
    )(queries, keys, values, cr, ct, *after)


def last_kernel(heads, gain_ref, p_ref, *rest):
    half, n = p_ref.shape[0], len(heads)
    attn_refs, q_refs = rest[:n], rest[n : 2 * n]
    out_ref, mark_ref, buf, sems = rest[-4:]
    mark_ref[...] = jnp.zeros(mark_ref.shape, f32)
    first = pl.multiple_of(((heads[0] + half * place()[0]) % (2 * half)) * 128, 128 * n)
    tokens = buf.shape[0]
    state = []
    for i in heads:
        hi, lo = split2(p_ref[i % half, 0:128, :])
        state.append((jnp.concatenate([hi, hi], axis=0), lo))
    copies = []
    for j in range(tokens // BLK):
        rows = slice(j * BLK, (j + 1) * BLK)
        for i in range(n):
            at = pl.multiple_of(first + i * 128, 128)
            both = q_refs[i][rows, :]
            carried = dot(both, state[i][0]) + dot(both[:, :128], state[i][1])
            attn = attn_refs[i][rows, :] + carried
            mean = jnp.mean(attn * attn, axis=1, keepdims=True)
            normed = attn * lax.rsqrt(mean + 1e-5) * gain_ref[:, pl.ds(at, 128)]
            buf[rows, i * 128 : (i + 1) * 128] = normed.astype(bf16)
        copy = pltpu.make_async_copy(buf.at[rows, :], out_ref.at[rows, pl.ds(first, n * 128)], sems.at[j])
        copy.start()
        copies.append(copy)
    for copy in copies:
        copy.wait()


def last_part(heads, gain, state, attn, scaled, out=None, after=()):
    n = len(heads)
    tokens, width = attn[0].shape[0], gain.shape[1]
    given = ([] if out is None else [out]) + list(after)
    return pl.pallas_call(
        functools.partial(last_kernel, heads),
        out_shape=[jax.ShapeDtypeStruct((tokens, width), bf16), jax.ShapeDtypeStruct((8, 128), f32)],
        in_specs=[VMEM] * (2 + 2 * n) + [ANY] * len(given),
        out_specs=[HBM, VMEM],
        scratch_shapes=[pltpu.VMEM((tokens, n * 128), bf16), pltpu.SemaphoreType.DMA((tokens // BLK,))],
        input_output_aliases={} if out is None else {2 + 2 * n: 0},
        compiler_params=PARAMS,
        cost_estimate=pl.CostEstimate(flops=n * tokens * 2 * 384 * 128, bytes_accessed=10 * tokens * 128 * n, transcendentals=tokens * n),
        name="last",
    )(gain, state, *[attn[i] for i in heads], *[scaled[i] for i in heads], *given)


def per_device(queries, keys, values, log_decay, out_gain, decode_map):
    ctx_size = lax.axis_size("ctx")
    head_size = lax.axis_size("head")

    def swap(a, mask):
        return lax.ppermute(a, "ctx", [(i, i ^ mask) for i in range(ctx_size)])

    def swap_y(a, mask):
        return lax.ppermute(a, "head", [(i, i ^ mask) for i in range(head_size)])

    tokens = queries.shape[0]
    heads = log_decay.shape[0]
    half = heads // 2
    ext = (128 + EXT, 128)
    send, keep, k_heads, v_heads = summaries(keys, values, log_decay, decode_map)
    recv = swap(send, 1)

    *t, want = small(pair_kernel, [ext] * 4 + [(8, 128)], "pair")(keep, recv)
    cr, ct = small(prep_kernel, [(heads, tokens), (tokens, heads)], "prep", (t[0],))(log_decay)
    attn, scaled = [None] * heads, [None] * heads

    def local(which, *after):
        got = local_part(which, queries, k_heads, v_heads, cr, ct, after)
        for n, i in enumerate(which):
            attn[i], scaled[i] = got[n], got[n + len(which)]
        return tuple(got[: len(which)])

    t = [t[0]] + [swap(a, 2 * d) for a, d in zip(t[1:], FAR_FIRST[1:])]
    done = local((0,), t[0])
    (g,) = small(slab_kernel, [ext], "slab", done)(*t)
    a = []
    plan = ((0, 8, (1, 2)), (1, 16, (3, 4)), (2, 48, (5, 6)))
    for bit, mask, which in plan:
        r = swap(g, mask)
        done = local(which, g)
        if bit == 0:
            want_y = swap_y(want, 1)
        if bit == 1:
            done = done + (want_y,)
        g, *a = small(functools.partial(round_kernel, bit), [ext] * 2, "round", done)(g, r, *a)
    m = small(back_kernel, [(256, 128)] * 4, "back")(g, *a, *t)
    (want_a,) = small(want_kernel, [(8, 128)], "want", (m[0],))(want, want_y)
    want_b = swap_y(want_a, 3)
    done = local((7,), m[0])
    m = [m[0]] + [swap(a, 2 * d) for a, d in zip(m[1:], FAR_FIRST[1:])]
    own, other, slots = small(
        spread_kernel, [(half, 128, 128), (half, 144, 128), (4, 16, 128)], "spread", done
    )(want_a, want_b, *m, keep, recv)
    other = swap(other, 1)

    gain = out_gain.reshape(1, -1)
    out, mark = last_part((0, 1), gain, own, attn, scaled)
    slot_send, near, far = small(merge_kernel, [(2, 16, 128), (16, 128), (16, 128)], "merge", (mark,))(slots, other)
    got = swap_y(slot_send, 1)
    out, mark = last_part((2, 3), gain, own, attn, scaled, out, (near,))
    near, far = small(slots_kernel, [(16, 128)] * 2, "slots", (mark,))(got, near, far)
    got = swap_y(far, 3)
    out, mark = last_part((4, 5, 6, 7), gain, other, attn, scaled, out, (near,))
    (decode_state,) = small(add_kernel, [(16, 128)], "sum", (mark,))(near, got)
    return (out, decode_state)


def solution(mesh):
    return jax.shard_map(
        per_device,
        mesh=mesh,
        in_specs=(
            P("ctx", "head"),
            P("ctx", "head"),
            P("ctx", "head"),
            P("head", "ctx"),
            P("head"),
            P(("ctx", "head")),
        ),
        out_specs=(P("ctx", "head"), P(("ctx", "head"), None)),
        check_vma=False,
    )
```

```python
import functools

import jax
import jax.numpy as jnp
from jax import lax
from jax.experimental import pallas as pl
from jax.experimental.pallas import tpu as pltpu
from jax.sharding import PartitionSpec as P

BLK = 256
EXT = 8
f32 = jnp.float32
bf16 = jnp.bfloat16
SMEM = pl.BlockSpec(memory_space=pltpu.SMEM)
VMEM = pl.BlockSpec(memory_space=pltpu.VMEM)
HBM = pl.BlockSpec(memory_space=pltpu.HBM)
ANY = pl.BlockSpec(memory_space=pl.ANY)
FAR_FIRST = (0, 2, 1, 3)
LOG2E = 1.4426950408889634
PARAMS = pltpu.CompilerParams(vmem_limit_bytes=40 * 1024 * 1024)


def dot(a, b):
    return lax.dot_general(a, b, (((1,), (0,)), ((), ())), preferred_element_type=f32)


def split2(x):
    hi = x.astype(bf16)
    return hi, (x - hi.astype(f32)).astype(bf16)


def split3(x):
    hi = x.astype(bf16)
    rest = x - hi.astype(f32)
    mid = rest.astype(bf16)
    return hi, mid, (rest - mid.astype(f32)).astype(bf16)


def block_cums(ld):
    heads, tokens = ld.shape
    n = tokens // BLK
    row = lax.broadcasted_iota(jnp.int32, (BLK, BLK), 0)
    col = lax.broadcasted_iota(jnp.int32, (BLK, BLK), 1)
    tri = jnp.where(row <= col, 1.0, 0.0).astype(bf16)
    parts = []
    for j in range(n):
        parts += list(split3(ld[:, j * BLK : (j + 1) * BLK].astype(f32)))
    stacked = jnp.concatenate([p.astype(f32) for p in parts], axis=0).astype(bf16)
    sums = dot(stacked, tri)
    out = []
    for j in range(n):
        a = sums[(3 * j) * heads : (3 * j + 1) * heads]
        b = sums[(3 * j + 1) * heads : (3 * j + 2) * heads]
        c = sums[(3 * j + 2) * heads : (3 * j + 3) * heads]
        out.append(a + (b + c))
    return out


def place():
    at = lax.axis_index("ctx")
    return at & 1, (at >> 1) & 3, at >> 3, lax.axis_index("head")


def kept_first(ld, core):
    half = ld.shape[0] // 2
    return jnp.where(core == 0, ld, jnp.concatenate([ld[half:], ld[:half]], axis=0))


def head_column(i, heads):
    return pl.multiple_of(((i + heads // 2 * place()[0]) % heads) * 128, 128)


def state_sum(k, v, w):
    kt = k.T.astype(f32) * w
    hi, lo = split2(kt)
    both = dot(jnp.concatenate([hi, lo], axis=0), v)
    return both[:128] + both[128:]


def write_sum(s_ref, i, state, tot_ref, h):
    s_ref[i, 0:128, :] = state
    heads = tot_ref.shape[0] - 8
    s_ref[i, 128:135, :] = jnp.broadcast_to(tot_ref[h : h + 1, :], (7, 128))
    s_ref[i, 135:136, :] = tot_ref[heads : heads + 1, :]


def send_kernel(k_hbm, v_hbm, ld_hbm, map_ref, s_ref, w_ref, tot_ref, k_ref, v_ref, ld_buf, sems, ld_sem):
    core = place()[0]
    heads, tokens = ld_buf.shape
    half = heads // 2
    ld_copy = pltpu.make_async_copy(ld_hbm, ld_buf, ld_sem)
    ld_copy.start()
    def fetch(side):
        cols = pl.ds(pl.multiple_of(((side + core) % 2) * half * 128, half * 128), half * 128)
        copies = []
        for r in range(sems.shape[2]):
            rows = pl.ds(r * (tokens // sems.shape[2]), tokens // sems.shape[2])
            for n, (src, buf) in enumerate(((k_hbm, k_ref), (v_hbm, v_ref))):
                copies.append(pltpu.make_async_copy(src.at[rows, cols], buf.at[rows, cols], sems.at[n, side, r]))
        for copy in copies:
            copy.start()
        return copies

    sent = fetch(1)
    ld_copy.wait()
    kept = fetch(0)
    ld = kept_first(ld_buf[...], core)
    n = tokens // BLK
    cums = block_cums(ld)
    after = jnp.zeros((heads, 1), f32)
    for j in reversed(range(n)):
        total = cums[j][:, BLK - 1 : BLK]
        w_ref[:, j * BLK : (j + 1) * BLK] = jnp.exp(total - cums[j] + after)
        after = after + total
    tot_ref[0:heads, :] = jnp.broadcast_to(after, (heads, 128))
    tot_ref[heads:, :] = jnp.full((8, 128), map_ref[0], jnp.int32).astype(f32)
    for copy in sent:
        copy.wait()
    for i in range(half):
        h = i + half
        cols = pl.ds(head_column(h, heads), 128)
        write_sum(s_ref, i, state_sum(k_ref[:, cols], v_ref[:, cols], w_ref[h : h + 1, :]), tot_ref, h)
    for copy in kept:
        copy.wait()


def keep_kernel(k_ref, v_ref, w_ref, tot_ref, s_ref):
    for i in range(s_ref.shape[0]):
        cols = pl.ds(head_column(i, 2 * s_ref.shape[0]), 128)
        write_sum(s_ref, i, state_sum(k_ref[:, cols], v_ref[:, cols], w_ref[i : i + 1, :]), tot_ref, i)


def summaries(keys, values, ld, decode_map):
    tokens, _ = keys.shape
    heads = ld.shape[0]
    half = heads // 2
    out = jax.ShapeDtypeStruct((half, 128 + EXT, 128), f32)
    cost = pl.CostEstimate(flops=2 * 2 * half * tokens * 128 * 128, bytes_accessed=2 * tokens * heads * 128, transcendentals=0)
    inputs = [pltpu.with_memory_space_constraint(a, pltpu.HBM) for a in (keys, values, ld)]
    send, w, tot, k_heads, v_heads = pl.pallas_call(
        send_kernel,
        out_shape=[
            out,
            jax.ShapeDtypeStruct((heads, tokens), f32),
            jax.ShapeDtypeStruct((heads + 8, 128), f32),
            jax.ShapeDtypeStruct(keys.shape, bf16),
            jax.ShapeDtypeStruct(keys.shape, bf16),
        ],
        in_specs=[HBM, HBM, HBM, SMEM],
        out_specs=[VMEM] * 5,
        scratch_shapes=[
            pltpu.VMEM((heads, tokens), f32),
            pltpu.SemaphoreType.DMA((2, 2, 1)),
            pltpu.SemaphoreType.DMA(()),
        ],
        compiler_params=PARAMS,
        cost_estimate=cost,
        name="summary_send",
    )(*inputs, decode_map)
    keep = pl.pallas_call(
        keep_kernel,
        out_shape=out,
        in_specs=[VMEM] * 4,
        out_specs=VMEM,
        compiler_params=PARAMS,
        cost_estimate=cost,
        name="summary_keep",
    )(k_heads, v_heads, w, tot)
    return send, keep, k_heads, v_heads


def compose(early, late):
    scale = jnp.exp(late[1])
    return (scale[0:1] * early[0] + late[0], early[1] + late[1])


def parts(ref):
    return (ref[0:128, :], ref[128:136, :])


def pair_kernel(keep_ref, recv_ref, *outs):
    core, x, _, _ = place()
    zero = core == 0
    for n, d in enumerate(FAR_FIRST):
        j = x ^ d
        own = (keep_ref[j, 0:128, :], keep_ref[j, 128:136, :])
        got = (recv_ref[j, 0:128, :], recv_ref[j, 128:136, :])
        early = tuple(jnp.where(zero, a, b) for a, b in zip(own, got))
        late = tuple(jnp.where(zero, b, a) for a, b in zip(own, got))
        state, decay = compose(early, late)
        outs[n][0:128, :] = state
        outs[n][128:136, :] = decay
    outs[4][0:1, :] = keep_ref[0, 135:136, :]
    outs[4][1:2, :] = recv_ref[0, 135:136, :]
    outs[4][2:8, :] = jnp.zeros((6, 128), f32)


def pick(x, j, refs):
    state, decay = parts(refs[0])
    for n in range(1, 4):
        here = (x ^ FAR_FIRST[n]) == j
        s, e = parts(refs[n])
        state, decay = jnp.where(here, s, state), jnp.where(here, e, decay)
    return state, decay


def slab_kernel(t0, t1, t2, t3, u_ref):
    _, x, _, _ = place()
    refs = (t0, t1, t2, t3)
    total = pick(x, 0, refs)
    for j in range(1, 4):
        total = compose(total, pick(x, j, refs))
    u_ref[0:128, :] = total[0]
    u_ref[128:136, :] = total[1]


def want_kernel(want_ref, got_ref, w_ref):
    w_ref[0:2, :] = want_ref[0:2, :]
    w_ref[2:4, :] = got_ref[0:2, :]
    w_ref[4:8, :] = jnp.zeros((4, 128), f32)


def round_kernel(bit, g_ref, r_ref, *rest):
    a_ref = rest[0] if len(rest) == 3 else None
    g_out, a_out = rest[-2:]
    late = ((place()[2] >> bit) & 1) == 1
    g, r = parts(g_ref), parts(r_ref)
    early_part = tuple(jnp.where(late, p, q) for p, q in zip(r, g))
    late_part = tuple(jnp.where(late, p, q) for p, q in zip(g, r))
    state, decay = compose(early_part, late_part)
    g_out[0:128, :] = state
    g_out[128:136, :] = decay
    a = parts(a_ref) if a_ref is not None else tuple(jnp.zeros_like(p) for p in r)
    state, decay = compose(r, a)
    a_out[0:128, :] = jnp.where(late, state, a[0])
    a_out[128:136, :] = jnp.where(late, decay, a[1])


def back_kernel(g_ref, a_ref, t0, t1, t2, t3, *outs):
    _, x, _, _ = place()
    refs = (t0, t1, t2, t3)
    before = [parts(a_ref)]
    for j in range(3):
        before.append(compose(before[-1], pick(x, j, refs)))
    for n, d in enumerate(FAR_FIRST):
        j = x ^ d
        state = before[0][0]
        for i in range(1, 4):
            state = jnp.where(j == i, before[i][0], state)
        outs[n][0:128, :] = state
        outs[n][128:256, :] = g_ref[0:128, :]


def spread_kernel(want_a, want_b, m0, m1, m2, m3, keep_ref, recv_ref, own_ref, send_ref, slot_ref):
    core, x, _, y = place()
    zero = core == 0
    refs = (m0, m1, m2, m3)
    for n, d in enumerate(FAR_FIRST):
        j = x ^ d
        chip = refs[n][0:128, :]
        s0 = jnp.where(zero, keep_ref[j, 0:128, :], recv_ref[j, 0:128, :])
        l0 = jnp.where(zero, keep_ref[j, 128:129, :], recv_ref[j, 128:129, :])
        second = jnp.exp(l0) * chip + s0
        own_ref[j] = jnp.where(zero, chip, second)
        send_ref[j, 0:128, :] = jnp.where(zero, second, chip)
    base = (y * 2 + core) * 32
    for slot in range(8):
        away = (0, 1, 3, 2)[slot // 2]
        want = (want_a if slot < 4 else want_b)[slot % 4 : slot % 4 + 1, :]
        rows = jnp.zeros((16, 128), f32)
        for n, d in enumerate(FAR_FIRST):
            for r in range(8):
                number = (base + (x ^ d) * 8 + r).astype(f32)
                rows = jnp.where(want == number, refs[n][128 + r * 16 : 144 + r * 16, :], rows)
        if slot % 2:
            send_ref[away, 128:144, :] = rows
        else:
            slot_ref[away] = rows


def merge_kernel(slot_ref, got_ref, send_ref, near_ref, far_ref):
    both = [slot_ref[d] + got_ref[d, 128:144, :] for d in range(4)]
    near_ref[...], far_ref[...] = both[0], both[3]
    send_ref[0], send_ref[1] = both[1], both[2]


def slots_kernel(got_ref, a_ref, b_ref, near_ref, far_ref):
    near_ref[...] = a_ref[...] + got_ref[0]
    far_ref[...] = b_ref[...] + got_ref[1]


def add_kernel(a_ref, b_ref, out_ref):
    out_ref[...] = a_ref[...] + b_ref[...]


def small(kernel, outs, name, after=()):
    def call(*args):
        def body(*refs):
            kernel(*refs[: len(args)], *refs[len(args) + len(after) :])

        return pl.pallas_call(
            body,
            out_shape=[jax.ShapeDtypeStruct(s, f32) for s in outs],
            in_specs=[VMEM] * len(args) + [ANY] * len(after),
            out_specs=[VMEM] * len(outs),
            compiler_params=PARAMS,
            name=name,
        )(*args, *after)

    return call


def prep_kernel(ld_ref, cr_ref, ct_ref):
    core = place()[0]
    ld = kept_first(ld_ref[...], core)
    for j, cum in enumerate(block_cums(ld)):
        rows = slice(j * BLK, (j + 1) * BLK)
        cum = cum * LOG2E
        cr_ref[:, rows] = cum
        ct_ref[rows, :] = cum.T


def local_kernel(heads, q_ref, k_ref, v_ref, cr_ref, ct_ref, *rest):
    total_heads, tokens = cr_ref.shape
    outs, scaled = rest[: len(heads)], rest[len(heads) :]
    h2 = BLK // 2
    row = lax.broadcasted_iota(jnp.int32, (h2, h2), 0)
    col = lax.broadcasted_iota(jnp.int32, (h2, h2), 1)
    causal = row >= col
    for i, out, qs in zip(heads, outs, scaled):
        at = head_column(i, total_heads)
        run = None
        off = jnp.zeros((1, 1), f32)
        for j in range(tokens // BLK):
            rows = slice(j * BLK, (j + 1) * BLK)
            q, k, v = q_ref[rows, pl.ds(at, 128)], k_ref[rows, pl.ds(at, 128)], v_ref[rows, pl.ds(at, 128)]
            c_row = cr_ref[i : i + 1, rows]
            c_col = ct_ref[rows, i : i + 1]
            total = c_row[:, BLK - 1 : BLK]
            decay = jnp.broadcast_to(jnp.exp2(c_col), (BLK, 128))
            hi, lo = split2(q.astype(f32) * (decay * jnp.exp2(off)))
            qs[rows, 0:128] = hi
            qs[rows, 128:256] = lo
            off = off + total
            scores = lax.dot_general(q, k, (((1,), (1,)), ((), ())), preferred_element_type=f32)
            gap = c_col - c_row
            top = jnp.where(causal, jnp.exp2(gap[:h2, :h2]) * scores[:h2, :h2], 0.0)
            low = jnp.exp2(gap[h2:, :h2]) * scores[h2:, :h2]
            end = jnp.where(causal, jnp.exp2(gap[h2:, h2:]) * scores[h2:, h2:], 0.0)
            left = jnp.concatenate([top.astype(bf16), low.astype(bf16)], axis=0)
            right = jnp.concatenate([jnp.zeros((h2, h2), bf16), end.astype(bf16)], axis=0)
            mixed = [jnp.concatenate([left, right], axis=1)]
            more = j + 1 < tokens // BLK
            if more:
                mixed += split2(k.T.astype(f32) * jnp.exp2(total - c_row))
            mixed = dot(jnp.concatenate(mixed, axis=0), v)
            attn = mixed[:BLK]
            if run is not None:
                attn = attn + dot(jnp.concatenate([q, q], axis=1), halves) * decay
            out[rows, :] = attn
            if more:
                new = mixed[BLK : BLK + 128] + mixed[BLK + 128 :]
                run = new if run is None else run * jnp.exp2(total) + new
                halves = jnp.concatenate(split2(run), axis=0)


def local_part(heads, queries, keys, values, cr, ct, after):
    tokens = queries.shape[0]
    n = len(heads)

    def body(*refs):
        local_kernel(heads, *refs[:5], *refs[5 + len(after) :])

    return pl.pallas_call(
        body,
        out_shape=[jax.ShapeDtypeStruct((tokens, 128), f32)] * n + [jax.ShapeDtypeStruct((tokens, 256), bf16)] * n,
        in_specs=[VMEM] * 5 + [ANY] * len(after),
        out_specs=[VMEM] * 2 * n,
        compiler_params=PARAMS,
        cost_estimate=pl.CostEstimate(flops=n * tokens * 2 * 128 * (256 + 256 + 256), bytes_accessed=10 * tokens * 128 * n, transcendentals=n * tokens * 200),
        name="local_attn",
    )(queries, keys, values, cr, ct, *after)


def last_kernel(heads, gain_ref, p_ref, *rest):
    half, n = p_ref.shape[0], len(heads)
    attn_refs, q_refs = rest[:n], rest[n : 2 * n]
    out_ref, mark_ref, buf, sems = rest[-4:]
    mark_ref[...] = jnp.zeros(mark_ref.shape, f32)
    first = pl.multiple_of(((heads[0] + half * place()[0]) % (2 * half)) * 128, 128 * n)
    tokens = buf.shape[0]
    state = []
    for i in heads:
        hi, lo = split2(p_ref[i % half, 0:128, :])
        state.append((jnp.concatenate([hi, hi], axis=0), lo))
    copies = []
    for j in range(tokens // BLK):
        rows = slice(j * BLK, (j + 1) * BLK)
        for i in range(n):
            at = pl.multiple_of(first + i * 128, 128)
            both = q_refs[i][rows, :]
            carried = dot(both, state[i][0]) + dot(both[:, :128], state[i][1])
            attn = attn_refs[i][rows, :] + carried
            mean = jnp.mean(attn * attn, axis=1, keepdims=True)
            normed = attn * lax.rsqrt(mean + 1e-5) * gain_ref[:, pl.ds(at, 128)]
            buf[rows, i * 128 : (i + 1) * 128] = normed.astype(bf16)
        copy = pltpu.make_async_copy(buf.at[rows, :], out_ref.at[rows, pl.ds(first, n * 128)], sems.at[j])
        copy.start()
        copies.append(copy)
    for copy in copies:
        copy.wait()


def last_part(heads, gain, state, attn, scaled, out=None, after=()):
    n = len(heads)
    tokens, width = attn[0].shape[0], gain.shape[1]
    given = ([] if out is None else [out]) + list(after)
    return pl.pallas_call(
        functools.partial(last_kernel, heads),
        out_shape=[jax.ShapeDtypeStruct((tokens, width), bf16), jax.ShapeDtypeStruct((8, 128), f32)],
        in_specs=[VMEM] * (2 + 2 * n) + [ANY] * len(given),
        out_specs=[HBM, VMEM],
        scratch_shapes=[pltpu.VMEM((tokens, n * 128), bf16), pltpu.SemaphoreType.DMA((tokens // BLK,))],
        input_output_aliases={} if out is None else {2 + 2 * n: 0},
        compiler_params=PARAMS,
        cost_estimate=pl.CostEstimate(flops=n * tokens * 2 * 384 * 128, bytes_accessed=10 * tokens * 128 * n, transcendentals=tokens * n),
        name="last",
    )(gain, state, *[attn[i] for i in heads], *[scaled[i] for i in heads], *given)


def per_device(queries, keys, values, log_decay, out_gain, decode_map):
    ctx_size = lax.axis_size("ctx")
    head_size = lax.axis_size("head")

    def swap(a, mask):
        return lax.ppermute(a, "ctx", [(i, i ^ mask) for i in range(ctx_size)])

    def swap_y(a, mask):
        return lax.ppermute(a, "head", [(i, i ^ mask) for i in range(head_size)])

    tokens = queries.shape[0]
    heads = log_decay.shape[0]
    half = heads // 2
    ext = (128 + EXT, 128)
    send, keep, k_heads, v_heads = summaries(keys, values, log_decay, decode_map)
    recv = swap(send, 1)

    cr, ct = small(prep_kernel, [(heads, tokens), (tokens, heads)], "prep", (keep,))(log_decay)
    *t, want = small(pair_kernel, [ext] * 4 + [(8, 128)], "pair", (cr,))(keep, recv)
    attn, scaled = [None] * heads, [None] * heads

    def local(which, *after):
        got = local_part(which, queries, k_heads, v_heads, cr, ct, after)
        for n, i in enumerate(which):
            attn[i], scaled[i] = got[n], got[n + len(which)]
        return tuple(got[: len(which)])

    t = [t[0]] + [swap(a, 2 * d) for a, d in zip(t[1:], FAR_FIRST[1:])]
    done = local((0,), t[0])
    (g,) = small(slab_kernel, [ext], "slab", done)(*t)
    a = []
    plan = ((0, 8, (1, 2)), (1, 16, (3, 4)), (2, 48, (5, 6)))
    for bit, mask, which in plan:
        r = swap(g, mask)
        done = local(which, g)
        if bit == 0:
            want_y = swap_y(want, 1)
        if bit == 1:
            done = done + (want_y,)
        g, *a = small(functools.partial(round_kernel, bit), [ext] * 2, "round", done)(g, r, *a)
    m = small(back_kernel, [(256, 128)] * 4, "back")(g, *a, *t)
    (want_a,) = small(want_kernel, [(8, 128)], "want", (m[0],))(want, want_y)
    want_b = swap_y(want_a, 3)
    done = local((7,), m[0])
    m = [m[0]] + [swap(a, 2 * d) for a, d in zip(m[1:], FAR_FIRST[1:])]
    own, other, slots = small(
        spread_kernel, [(half, 128, 128), (half, 144, 128), (4, 16, 128)], "spread", done
    )(want_a, want_b, *m, keep, recv)
    other = swap(other, 1)

    gain = out_gain.reshape(1, -1)
    slot_send, near, far = small(merge_kernel, [(2, 16, 128), (16, 128), (16, 128)], "merge")(slots, other)
    got = swap_y(slot_send, 1)
    out, mark = last_part((0, 1, 2, 3), gain, own, attn, scaled, None, (near,))
    near, far = small(slots_kernel, [(16, 128)] * 2, "slots", (mark,))(got, near, far)
    got = swap_y(far, 3)
    out, mark = last_part((4, 5, 6, 7), gain, other, attn, scaled, out, (near,))
    (decode_state,) = small(add_kernel, [(16, 128)], "sum", (mark,))(near, got)
    return (out, decode_state)


def solution(mesh):
    return jax.shard_map(
        per_device,
        mesh=mesh,
        in_specs=(
            P("ctx", "head"),
            P("ctx", "head"),
            P("ctx", "head"),
            P("head", "ctx"),
            P("head"),
            P(("ctx", "head")),
        ),
        out_specs=(P("ctx", "head"), P(("ctx", "head"), None)),
        check_vma=False,
    )
```
